256 devices in a mesh: blk: 16 (over y_lo, x, core), width: 16 (over y_hi, z).
Axes of the slice: x: 4, y: 4 (y_hi: 2, y_lo: 2; y = y_hi * 2 + y_lo), z: 8, core: 2. Of those that a mesh axis runs over, the one named last changes fastest.
Arguments:
- inputs: bfloat16 [16, 128, 2048], P('blk', None, 'width'), may hold values from -6 to 6
- encoder: bfloat16 [16, 2048, 4096], P('blk', 'width'), may hold values from -0.125 to 0.125
- enc_bias: float32 [16, 4096], P('blk'), may hold values from -3 to 3
- active_blocks: int32 [16, 128, 32], P('blk'), may hold values 0 or 1
- near_decoders: bfloat16 [16, 8, 4096, 2048], P('blk', None, None, 'width'), may hold values from -0.09375 to 0.09375
- far_decoders: bfloat16 [16, 2048, 2048], P('blk', None, 'width'), may hold values from -0.09375 to 0.09375
- targets: bfloat16 [16, 128, 2048], P('blk', None, 'width'), may hold values from -6 to 6
Outputs:
- reconstruction: float32 [16, 128, 2048], P('blk', None, 'width')
- grad_encoder: bfloat16 [16, 2048, 4096], P('blk', 'width')
- grad_bias: float32 [16, 4096], P('blk')
The draws below stay inside these ranges and needn't reach their ends.
All inputs are finite; a program needn't handle non-finite values. No bound on the sum of `active_blocks` on one device may be relied on, other than what follows from the above.
Results may differ from the reference program's by a relative error of at most 0.011.
Values may be sent and summed in bfloat16 or wider, within the bound.
No kernel may reach another device: no remote copies, remote signals or barrier semaphores. Data moves between devices by JAX's collectives and lax.ppermute only.
A program may use at most 128 MiB of HBM per device.

```python
import jax
import jax.numpy as jnp

D = 2048
F = 4096
FBLK = 128
TOK = 128
LAYERS = 16
NEAR = 8
FB = 32


def plant(values, rng, smallest, largest):
    place = [jax.random.randint(jax.random.fold_in(rng, axis), (), 0, length) for axis, length in enumerate(values.shape)]
    main_axis = values.shape.index(max(values.shape))
    neighbour = place[:main_axis] + [(place[main_axis] + 1) % values.shape[main_axis]] + place[main_axis + 1:]
    return values.at[tuple(place)].set(smallest).at[tuple(neighbour)].set(largest)


def block_levels(stream_key, shape, split, least, high):
    level, own = 1.0, jax.random.fold_in(stream_key, 6)
    for dim, shards_of in split:
        heights = jnp.exp(jax.random.uniform(jax.random.fold_in(own, dim), (shards_of,), jnp.float32, least / len(split), high / len(split)))
        level = level * jnp.repeat(heights, shape[dim] // shards_of).reshape([-1 if axis == dim else 1 for axis in range(len(shape))])
    return level


def gaussian(own_key, dims, width, reach, shards=(), kind=jnp.bfloat16):
    entries = width * jax.random.normal(own_key, dims, jnp.float32)
    if shards:
        entries = entries * block_levels(own_key, dims, shards, -0.22, 0.18)
    return jnp.clip(entries, -reach, reach).astype(kind)


def setup_inputs(seed: int = 0) -> dict:
    arg_keys = jax.random.split(jax.random.key(seed), 8)
    inputs = gaussian(arg_keys[0], (LAYERS, TOK, D), 1.0, 6.0, ((0, 16), (2, 16)))
    encoder = gaussian(arg_keys[1], (LAYERS, D, F), D ** -0.5, 0.125, ((0, 16), (1, 16)))
    enc_bias = gaussian(arg_keys[2], (LAYERS, F), 0.5, 3.0, ((0, 16),), jnp.float32)
    active_blocks = plant((jax.random.randint(arg_keys[3], (LAYERS, TOK, FB), 0, 2) < 1).astype(jnp.int32), jax.random.fold_in(arg_keys[3], 1), 0, 1)
    near_decoders = gaussian(arg_keys[4], (LAYERS, NEAR, F, D), F ** -0.5, 0.09375, ((0, 16), (3, 16)))
    far_decoders = gaussian(arg_keys[5], (LAYERS, F // 2, D), F ** -0.5, 0.09375, ((0, 16), (2, 16)))
    targets = gaussian(arg_keys[6], (LAYERS, TOK, D), 1.0, 6.0, ((0, 16), (2, 16)))
    return {"inputs": inputs, "encoder": encoder, "enc_bias": enc_bias, "active_blocks": active_blocks, "near_decoders": near_decoders, "far_decoders": far_decoders, "targets": targets}


def expand_mask(blocks):
    return jnp.repeat(blocks.astype(jnp.float32), FBLK, axis=-1)


def pair_decoder(near_decoders, far_decoders, lower, upper):
    layers = LAYERS
    near_count = layers // 2
    spread = upper - lower
    if spread < near_count:
        return near_decoders[upper, spread]
    if spread == near_count:
        return jnp.concatenate([far_decoders[lower], far_decoders[upper]], axis=0)
    return near_decoders[lower, lower + layers - upper]


def reference(inputs, encoder, enc_bias, active_blocks, near_decoders, far_decoders, targets):
    layers = LAYERS
    masks_all = [expand_mask(active_blocks[level]) for level in range(layers)]
    activations = []
    for level in range(layers):
        pre_value = jnp.dot(inputs[level], encoder[level], preferred_element_type=jnp.float32) + enc_bias[level]
        activations.append((masks_all[level] * pre_value).astype(jnp.bfloat16))
    recon_rows = []
    out_grads = []
    for upper in range(layers):
        total = jnp.zeros((TOK, D), jnp.float32)
        for lower in range(upper + 1):
            weights = pair_decoder(near_decoders, far_decoders, lower, upper)
            total = total + jnp.dot(activations[lower], weights, preferred_element_type=jnp.float32)
        recon_rows.append(total)
        out_grads.append((total - targets[upper].astype(jnp.float32)).astype(jnp.bfloat16))
    enc_grads = []
    bias_grads = []
    for lower in range(layers):
        total = jnp.zeros((TOK, F), jnp.float32)
        for upper in range(lower, layers):
            weights = pair_decoder(near_decoders, far_decoders, lower, upper)
            total = total + jnp.dot(out_grads[upper], weights.T, preferred_element_type=jnp.float32)
        pre_grad = (masks_all[lower] * total).astype(jnp.bfloat16)
        enc_grads.append(jnp.dot(inputs[lower].T, pre_grad, preferred_element_type=jnp.float32).astype(jnp.bfloat16))
        bias_grads.append(jnp.sum(pre_grad.astype(jnp.float32), axis=0))
    return jnp.stack(recon_rows), jnp.stack(enc_grads), jnp.stack(bias_grads)
```

```python
import functools

import jax
import jax.numpy as jnp
from jax import lax
from jax.experimental import pallas as pl
from jax.experimental.pallas import tpu as pltpu
from jax.sharding import PartitionSpec as P

FBLK = 128
BF16 = jnp.bfloat16
F32 = jnp.float32
SMEM = pltpu.MemorySpace.SMEM
VMEM_LIMIT = 40 * 1024 * 1024


def exchange(parts, axis):
    return lax.all_to_all(parts, axis, 0, 0, tiled=True)


def shifted_down(block, distance, lowest=0):
    count = lax.axis_size("blk")
    route = [(i, i - distance) for i in range(count) if i - distance >= lowest]
    return lax.ppermute(block, "blk", route)


def pre_kernel(in_ref, enc_ref, out_ref):
    columns = out_ref.shape[2]
    product = jnp.dot(in_ref[...], enc_ref[...], preferred_element_type=F32)
    for part in range(out_ref.shape[0]):
        out_ref[part] = product[:, part * columns : (part + 1) * columns].astype(BF16)


def pre_parts(local_in, encoder, parts):
    tokens, rows = local_in.shape
    features = encoder.shape[1]
    columns = features // parts
    step = 4
    return pl.pallas_call(
        pre_kernel,
        grid=(parts // step,),
        in_specs=[
            pl.BlockSpec((tokens, rows), lambda c: (0, 0)),
            pl.BlockSpec((rows, step * columns), lambda c: (0, c)),
        ],
        out_specs=pl.BlockSpec((step, tokens, columns), lambda c: (c, 0, 0)),
        out_shape=jax.ShapeDtypeStruct((parts, tokens, columns), BF16),
        name="pre_parts",
    )(local_in, encoder)


def masked_sum_kernel(parts_ref, bias_ref, blocks_ref, out_ref):
    count, tokens, columns = parts_ref.shape
    total = parts_ref[0].astype(F32)
    for part in range(1, count):
        total = total + parts_ref[part].astype(F32)
    total = total + bias_ref[...]
    blocks = blocks_ref[...].astype(F32)
    mask = jnp.concatenate(
        [
            jnp.broadcast_to(blocks[:, b : b + 1], (tokens, FBLK))
            for b in range(columns // FBLK)
        ],
        axis=1,
    )
    value = (mask * total).astype(BF16)
    for part in range(count):
        out_ref[part] = value


def masked_sum(parts, bias, blocks):
    return pl.pallas_call(
        masked_sum_kernel,
        out_shape=jax.ShapeDtypeStruct(parts.shape, BF16),
        name="masked_sum",
    )(parts, bias, blocks)


def weight_specs(near_shape, far_shape, chunk):
    slots, features, cols = near_shape
    far_chunks = far_shape[0] // chunk
    specs = [pl.BlockSpec((slots, chunk, cols), lambda c, *_: (0, c, 0))]
    specs += [pl.BlockSpec((chunk, cols), lambda c, *_: (c, 0))] * (slots - 1)
    specs += [
        pl.BlockSpec((chunk, cols), lambda c, *_: (jnp.minimum(c, far_chunks - 1), 0)),
        pl.BlockSpec((chunk, cols), lambda c, *_: (jnp.maximum(c - far_chunks, 0), 0)),
    ]
    return specs


def decoders_up(step, near_ref, moved_refs, far_ref, far_moved_ref, far_chunks):
    slots = near_ref.shape[0]
    found = [near_ref[0]] + [ref[...] for ref in moved_refs]
    found.append(jnp.where(step < far_chunks, far_ref[...], far_moved_ref[...]))
    found += [near_ref[2 * slots - r] for r in range(slots + 1, 2 * slots)]
    return found


def forward_kernel(far_chunks, place_ref, acts_ref, near_ref, *refs):
    slots = near_ref.shape[0]
    moved_refs, (far_ref, far_moved_ref, out_ref, total_ref) = refs[: slots - 1], refs[slots - 1 :]
    step = pl.program_id(0)
    layers = 2 * slots
    cols = near_ref.shape[2]

    @pl.when(step == 0)
    def _():
        total_ref[...] = jnp.zeros_like(total_ref)

    acts = jnp.concatenate([acts_ref[p] for p in range(acts_ref.shape[0])], axis=1)
    weights = decoders_up(step, near_ref, moved_refs, far_ref, far_moved_ref, far_chunks)
    for pair in range(slots):
        both = jnp.concatenate(weights[2 * pair : 2 * pair + 2], axis=1)
        total_ref[pair] += jnp.dot(acts, both, preferred_element_type=F32)

    @pl.when(step == pl.num_programs(0) - 1)
    def _():
        place = place_ref[0]
        for r in range(layers):
            share = total_ref[r // 2, :, (r % 2) * cols : (r % 2 + 1) * cols]
            kept = jnp.where(place + r < layers, share, 0.0)
            out_ref[lax.rem(place + r, layers)] = kept.astype(BF16)


def forward_shares(place, acts, near, moved, far, far_moved, chunk=512):
    slots, features, cols = near.shape
    parts, tokens, columns = acts.shape
    layers = 2 * slots
    return pl.pallas_call(
        functools.partial(forward_kernel, far.shape[0] // chunk),
        grid=(features // chunk,),
        in_specs=[
            pl.BlockSpec(memory_space=SMEM),
            pl.BlockSpec((chunk // columns, tokens, columns), lambda c: (c, 0, 0)),
            *weight_specs(near.shape, far.shape, chunk),
        ],
        out_specs=pl.BlockSpec((layers, tokens, cols), lambda c: (0, 0, 0)),
        out_shape=jax.ShapeDtypeStruct((layers, tokens, cols), BF16),
        scratch_shapes=[pltpu.VMEM((slots, tokens, 2 * cols), F32)],
        compiler_params=pltpu.CompilerParams(vmem_limit_bytes=VMEM_LIMIT),
        name="forward_shares",
    )(place, acts, near, *moved, far, far_moved)


def residual_kernel(shares_ref, target_ref, rec_ref, grads_ref):
    total = shares_ref[0].astype(F32)
    for part in range(1, shares_ref.shape[0]):
        total = total + shares_ref[part].astype(F32)
    rec_ref[...] = total
    grad = (total - target_ref[...].astype(F32)).astype(BF16)
    for part in range(grads_ref.shape[0]):
        grads_ref[part] = grad


def residual(shares, target):
    return pl.pallas_call(
        residual_kernel,
        out_shape=(
            jax.ShapeDtypeStruct(target.shape, F32),
            jax.ShapeDtypeStruct(shares.shape, BF16),
        ),
        name="residual",
    )(shares, target)


def backward_kernel(far_chunks, place_ref, grads_ref, near_ref, *refs):
    slots = near_ref.shape[0]
    moved_refs, (far_ref, far_moved_ref, out_ref, up_ref) = refs[: slots - 1], refs[slots - 1 :]
    step = pl.program_id(0)
    layers = 2 * slots
    cols = near_ref.shape[2]
    columns = out_ref.shape[2]

    @pl.when(step == 0)
    def _():
        place = place_ref[0]
        for r in range(layers):
            grad = grads_ref[lax.rem(place + r, layers)]
            up_ref[:, r * cols : (r + 1) * cols] = jnp.where(
                place + r < layers, grad, jnp.zeros_like(grad)
            )

    weights = decoders_up(step, near_ref, moved_refs, far_ref, far_moved_ref, far_chunks)
    product = lax.dot_general(
        up_ref[...],
        jnp.concatenate(weights, axis=1),
        (((1,), (1,)), ((), ())),
        preferred_element_type=F32,
    )
    for part in range(out_ref.shape[0]):
        out_ref[part] = product[:, part * columns : (part + 1) * columns].astype(BF16)


def backward_parts(place, grads, near, moved, far, far_moved, parts, chunk=512):
    slots, features, cols = near.shape
    layers, tokens, _ = grads.shape
    columns = features // parts
    return pl.pallas_call(
        functools.partial(backward_kernel, far.shape[0] // chunk),
        grid=(features // chunk,),
        in_specs=[
            pl.BlockSpec(memory_space=SMEM),
            pl.BlockSpec(grads.shape, lambda c: (0, 0, 0)),
            *weight_specs(near.shape, far.shape, chunk),
        ],
        out_specs=pl.BlockSpec((chunk // columns, tokens, columns), lambda c: (c, 0, 0)),
        out_shape=jax.ShapeDtypeStruct((parts, tokens, columns), BF16),
        scratch_shapes=[pltpu.VMEM((tokens, layers * cols), BF16)],
        compiler_params=pltpu.CompilerParams(vmem_limit_bytes=VMEM_LIMIT),
        name="backward_parts",
    )(place, grads, near, *moved, far, far_moved)


def encoder_grad_kernel(in_ref, pre_ref, enc_ref, bias_ref):
    columns = pre_ref.shape[2]
    for part in range(pre_ref.shape[0]):
        grad = pre_ref[part]
        span = slice(part * columns, (part + 1) * columns)
        enc_ref[:, span] = lax.dot_general(
            in_ref[...], grad, (((0,), (0,)), ((), ())), preferred_element_type=F32
        ).astype(BF16)
        bias_ref[:, span] = jnp.sum(grad.astype(F32), axis=0, keepdims=True)


def encoder_grads(local_in, pre_grad):
    tokens, rows = local_in.shape
    parts, _, columns = pre_grad.shape
    step = 4
    return pl.pallas_call(
        encoder_grad_kernel,
        grid=(parts // step,),
        in_specs=[
            pl.BlockSpec((tokens, rows), lambda c: (0, 0)),
            pl.BlockSpec((step, tokens, columns), lambda c: (c, 0, 0)),
        ],
        out_specs=[
            pl.BlockSpec((rows, step * columns), lambda c: (0, c)),
            pl.BlockSpec((1, step * columns), lambda c: (0, c)),
        ],
        out_shape=(
            jax.ShapeDtypeStruct((rows, parts * columns), BF16),
            jax.ShapeDtypeStruct((1, parts * columns), F32),
        ),
        name="encoder_grads",
    )(local_in, pre_grad)


EARLY = (1, 2, 3, 4)


def on_device(inputs, encoder, enc_bias, active_blocks, near_decoders, far_decoders, targets):
    parts = lax.axis_size("width")
    slots = near_decoders.shape[1]
    place = lax.axis_index("blk")[None].astype(jnp.int32)
    column = lax.axis_index("width")
    local_in = inputs[0]
    near, far = near_decoders[0], far_decoders[0]
    columns = encoder.shape[2] // parts
    per_part = columns // FBLK
    blocks = lax.dynamic_slice_in_dim(active_blocks[0], column * per_part, per_part, 1)
    bias = lax.dynamic_slice_in_dim(enc_bias, column * columns, columns, 1)

    moved = {o: shifted_down(near[o], o) for o in range(1, slots)}
    far_moved = shifted_down(far, slots)

    arrived = exchange(pre_parts(local_in, encoder[0], parts), "width")
    act_part = masked_sum(arrived, bias, blocks)
    early = [moved[o] for o in EARLY]
    act_part, early = lax.optimization_barrier((act_part, early))
    moved.update(zip(EARLY, early))
    acts = exchange(act_part, "width")
    moved = [moved[o] for o in range(1, slots)]
    shares = forward_shares(place, acts, near, moved, far, far_moved)
    reconstruction, own_grads = residual(exchange(shares, "blk"), targets[0])
    all_grads = exchange(own_grads, "blk")
    grad_parts = backward_parts(place, all_grads, near, moved, far, far_moved, parts)
    pre_part = masked_sum(exchange(grad_parts, "width"), jnp.zeros_like(bias), blocks)
    enc_grad, bias_grad = encoder_grads(local_in, exchange(pre_part, "width"))
    return reconstruction[None], enc_grad[None], bias_grad


def solution(mesh):
    return jax.shard_map(
        on_device,
        mesh=mesh,
        in_specs=(
            P("blk", None, "width"),
            P("blk", "width", None),
            P("blk", None),
            P("blk", None, None),
            P("blk", None, None, "width"),
            P("blk", None, "width"),
            P("blk", None, "width"),
        ),
        out_specs=(P("blk", None, "width"), P("blk", "width", None), P("blk", None)),
        check_vma=False,
    )
```

```python
import functools

import jax
import jax.numpy as jnp
from jax import lax
from jax.experimental import pallas as pl
from jax.experimental.pallas import tpu as pltpu
from jax.sharding import PartitionSpec as P

FBLK = 128
BF16 = jnp.bfloat16
F32 = jnp.float32
HALVES = 2
SMEM = pltpu.MemorySpace.SMEM
VMEM_LIMIT = 40 * 1024 * 1024


def exchange(parts, axis, runs=1):
    count = lax.axis_size(axis) // runs
    groups = [list(range(r * count, (r + 1) * count)) for r in range(runs)]
    return lax.all_to_all(parts, axis, 0, 0, tiled=True, axis_index_groups=groups)


def crossed(low, high, layers):
    spread = high - low
    half = layers // 2
    return (low < half) & (high >= half) & (low % 2 == 1) & (spread < half)


def shifted_down(block, distance):
    layers, parts = lax.axis_size("blk"), lax.axis_size("width")
    route = []
    for high in range(distance, layers):
        low = high - distance
        turn = parts // 2 if crossed(low, high, layers) else 0
        for part in range(parts):
            route.append((high * parts + part, low * parts + (part + turn) % parts))
    return lax.ppermute(block, ("blk", "width"), route)


def other_half(block):
    parts = lax.axis_size("width")
    return lax.ppermute(block, "width", [(p, (p + parts // 2) % parts) for p in range(parts)])


def pre_kernel(in_ref, enc_ref, out_ref):
    columns = out_ref.shape[2]
    product = jnp.dot(in_ref[...], enc_ref[...], preferred_element_type=F32)
    for part in range(out_ref.shape[0]):
        out_ref[part] = product[:, part * columns : (part + 1) * columns].astype(BF16)


def pre_parts(local_in, encoder, parts):
    tokens, rows = local_in.shape
    features = encoder.shape[1]
    columns = features // parts
    step = 2
    return pl.pallas_call(
        pre_kernel,
        grid=(parts // step,),
        in_specs=[
            pl.BlockSpec((tokens, rows), lambda c: (0, 0)),
            pl.BlockSpec((rows, step * columns), lambda c: (0, c)),
        ],
        out_specs=pl.BlockSpec((step, tokens, columns), lambda c: (c, 0, 0)),
        out_shape=jax.ShapeDtypeStruct((parts, tokens, columns), BF16),
        name="pre_parts",
    )(local_in, encoder)


def part_sum_kernel(parts_ref, out_ref):
    total = parts_ref[0].astype(F32)
    for part in range(1, parts_ref.shape[0]):
        total = total + parts_ref[part].astype(F32)
    out_ref[...] = total.astype(BF16)


def part_sum(parts):
    return pl.pallas_call(
        part_sum_kernel,
        out_shape=jax.ShapeDtypeStruct(parts.shape[1:], BF16),
        name="part_sum",
    )(parts)


def masked_sum_kernel(own_ref, came_ref, bias_ref, blocks_ref, out_ref):
    tokens, columns = own_ref.shape
    total = own_ref[...].astype(F32) + came_ref[...].astype(F32) + bias_ref[...]
    blocks = blocks_ref[...].astype(F32)
    mask = jnp.concatenate(
        [
            jnp.broadcast_to(blocks[:, b : b + 1], (tokens, FBLK))
            for b in range(columns // FBLK)
        ],
        axis=1,
    )
    value = (mask * total).astype(BF16)
    for part in range(out_ref.shape[0]):
        out_ref[part] = value


def masked_sum(own, came, bias, blocks, parts):
    return pl.pallas_call(
        masked_sum_kernel,
        out_shape=jax.ShapeDtypeStruct((parts, *own.shape), BF16),
        name="masked_sum",
    )(own, came, bias, blocks)


def summed_over_width(parts, bias, blocks):
    own = part_sum(exchange(parts, "width", HALVES))
    return exchange(masked_sum(own, other_half(own), bias, blocks, parts.shape[0]), "width", HALVES)


def weight_specs(near_shape, far_shape, chunk):
    slots, features, cols = near_shape
    far_chunks = far_shape[0] // chunk
    specs = [pl.BlockSpec((slots, chunk, cols), lambda c, *_: (0, c, 0))]
    specs += [pl.BlockSpec((chunk, cols), lambda c, *_: (c, 0))] * (slots - 1)
    specs += [
        pl.BlockSpec((chunk, cols), lambda c, *_: (jnp.minimum(c, far_chunks - 1), 0)),
        pl.BlockSpec((chunk, cols), lambda c, *_: (jnp.maximum(c - far_chunks, 0), 0)),
    ]
    return specs


def decoders_up(step, near_ref, moved_refs, far_ref, far_moved_ref, far_chunks):
    slots = near_ref.shape[0]
    found = [near_ref[0]] + [ref[...] for ref in moved_refs]
    found.append(jnp.where(step < far_chunks, far_ref[...], far_moved_ref[...]))
    found += [near_ref[2 * slots - r] for r in range(slots + 1, 2 * slots)]
    return found


def forward_kernel(far_chunks, place_ref, acts_ref, near_ref, *refs):
    slots = near_ref.shape[0]
    moved_refs, (far_ref, far_moved_ref, out_ref, total_ref) = refs[: slots - 1], refs[slots - 1 :]
    step = pl.program_id(0)
    layers = 2 * slots
    cols = near_ref.shape[2]

    @pl.when(step == 0)
    def _():
        total_ref[...] = jnp.zeros_like(total_ref)

    acts = jnp.concatenate([acts_ref[p] for p in range(acts_ref.shape[0])], axis=1)
    weights = decoders_up(step, near_ref, moved_refs, far_ref, far_moved_ref, far_chunks)
    for pair in range(slots):
        both = jnp.concatenate(weights[2 * pair : 2 * pair + 2], axis=1)
        total_ref[pair] += jnp.dot(acts, both, preferred_element_type=F32)

    @pl.when(step == pl.num_programs(0) - 1)
    def _():
        place = place_ref[0]
        for r in range(layers):
            share = total_ref[r // 2, :, (r % 2) * cols : (r % 2 + 1) * cols]
            kept = jnp.where(place + r < layers, share, 0.0)
            out_ref[lax.rem(place + r, layers)] = kept.astype(BF16)


def forward_shares(place, acts, near, moved, far, far_moved, chunk=512):
    slots, features, cols = near.shape
    parts, tokens, columns = acts.shape
    layers = 2 * slots
    return pl.pallas_call(
        functools.partial(forward_kernel, far.shape[0] // chunk),
        grid=(features // chunk,),
        in_specs=[
            pl.BlockSpec(memory_space=SMEM),
            pl.BlockSpec((chunk // columns, tokens, columns), lambda c: (c, 0, 0)),
            *weight_specs(near.shape, far.shape, chunk),
        ],
        out_specs=pl.BlockSpec((layers, tokens, cols), lambda c: (0, 0, 0)),
        out_shape=jax.ShapeDtypeStruct((layers, tokens, cols), BF16),
        scratch_shapes=[pltpu.VMEM((slots, tokens, 2 * cols), F32)],
        compiler_params=pltpu.CompilerParams(vmem_limit_bytes=VMEM_LIMIT),
        name="forward_shares",
    )(place, acts, near, *moved, far, far_moved)


def share_sums_kernel(place_ref, shares_ref, own_ref, other_ref, sent_ref):
    layers = shares_ref.shape[0]
    place = place_ref[0]
    own = jnp.zeros(own_ref.shape, F32)
    other = jnp.zeros(own_ref.shape, F32)
    for low in range(layers):
        share = shares_ref[low].astype(F32)
        away = crossed(low, place, layers)
        own = own + jnp.where(away, 0.0, share)
        other = other + jnp.where(away, share, 0.0)
    own_ref[...] = own
    other_ref[...] = other
    sent_ref[0] = own.astype(BF16)
    sent_ref[1] = other.astype(BF16)


def share_sums(place, shares):
    _, tokens, cols = shares.shape
    return pl.pallas_call(
        share_sums_kernel,
        in_specs=[pl.BlockSpec(memory_space=SMEM), pl.BlockSpec(memory_space=pltpu.VMEM)],
        out_shape=(
            jax.ShapeDtypeStruct((tokens, cols), F32),
            jax.ShapeDtypeStruct((tokens, cols), F32),
            jax.ShapeDtypeStruct((2, tokens, cols), BF16),
        ),
        name="share_sums",
    )(place, shares)


def residual_kernel(place_ref, own_ref, other_ref, came_ref, target_ref, away_target_ref, rec_ref, grads_ref):
    layers = grads_ref.shape[0]
    place = place_ref[0]
    rec = own_ref[...] + came_ref[1].astype(F32)
    away_rec = other_ref[...] + came_ref[0].astype(F32)
    rec_ref[...] = rec
    grad = (rec - target_ref[...].astype(F32)).astype(BF16)
    away_grad = (away_rec - away_target_ref[...].astype(F32)).astype(BF16)
    for low in range(layers):
        grads_ref[low] = jnp.where(crossed(low, place, layers), away_grad, grad)


def residual(place, own, other, came, target, away_target):
    layers = lax.axis_size("blk")
    vmem = pl.BlockSpec(memory_space=pltpu.VMEM)
    return pl.pallas_call(
        residual_kernel,
        in_specs=[pl.BlockSpec(memory_space=SMEM)] + [vmem] * 5,
        out_shape=(
            jax.ShapeDtypeStruct(target.shape, F32),
            jax.ShapeDtypeStruct((layers, *target.shape), BF16),
        ),
        name="residual",
    )(place, own, other, came, target, away_target)


def backward_kernel(far_chunks, place_ref, grads_ref, near_ref, *refs):
    slots = near_ref.shape[0]
    moved_refs, (far_ref, far_moved_ref, out_ref, up_ref) = refs[: slots - 1], refs[slots - 1 :]
    step = pl.program_id(0)
    layers = 2 * slots
    cols = near_ref.shape[2]
    columns = out_ref.shape[2]

    @pl.when(step == 0)
    def _():
        place = place_ref[0]
        for r in range(layers):
            grad = grads_ref[lax.rem(place + r, layers)]
            up_ref[:, r * cols : (r + 1) * cols] = jnp.where(
                place + r < layers, grad, jnp.zeros_like(grad)
            )

    weights = decoders_up(step, near_ref, moved_refs, far_ref, far_moved_ref, far_chunks)
    product = lax.dot_general(
        up_ref[...],
        jnp.concatenate(weights, axis=1),
        (((1,), (1,)), ((), ())),
        preferred_element_type=F32,
    )
    for part in range(out_ref.shape[0]):
        out_ref[part] = product[:, part * columns : (part + 1) * columns].astype(BF16)


def backward_parts(place, grads, near, moved, far, far_moved, parts, chunk=512):
    slots, features, cols = near.shape
    layers, tokens, _ = grads.shape
    columns = features // parts
    return pl.pallas_call(
        functools.partial(backward_kernel, far.shape[0] // chunk),
        grid=(features // chunk,),
        in_specs=[
            pl.BlockSpec(memory_space=SMEM),
            pl.BlockSpec(grads.shape, lambda c: (0, 0, 0)),
            *weight_specs(near.shape, far.shape, chunk),
        ],
        out_specs=pl.BlockSpec((chunk // columns, tokens, columns), lambda c: (c, 0, 0)),
        out_shape=jax.ShapeDtypeStruct((parts, tokens, columns), BF16),
        scratch_shapes=[pltpu.VMEM((tokens, layers * cols), BF16)],
        compiler_params=pltpu.CompilerParams(vmem_limit_bytes=VMEM_LIMIT),
        name="backward_parts",
    )(place, grads, near, *moved, far, far_moved)


def encoder_grad_kernel(in_ref, pre_ref, enc_ref, bias_ref):
    columns = pre_ref.shape[2]
    for part in range(pre_ref.shape[0]):
        grad = pre_ref[part]
        span = slice(part * columns, (part + 1) * columns)
        enc_ref[:, span] = lax.dot_general(
            in_ref[...], grad, (((0,), (0,)), ((), ())), preferred_element_type=F32
        ).astype(BF16)
        bias_ref[:, span] = jnp.sum(grad.astype(F32), axis=0, keepdims=True)


def encoder_grads(local_in, pre_grad):
    tokens, rows = local_in.shape
    parts, _, columns = pre_grad.shape
    step = 2
    return pl.pallas_call(
        encoder_grad_kernel,
        grid=(parts // step,),
        in_specs=[
            pl.BlockSpec((tokens, rows), lambda c: (0, 0)),
            pl.BlockSpec((step, tokens, columns), lambda c: (c, 0, 0)),
        ],
        out_specs=[
            pl.BlockSpec((rows, step * columns), lambda c: (0, c)),
            pl.BlockSpec((1, step * columns), lambda c: (0, c)),
        ],
        out_shape=(
            jax.ShapeDtypeStruct((rows, parts * columns), BF16),
            jax.ShapeDtypeStruct((1, parts * columns), F32),
        ),
        name="encoder_grads",
    )(local_in, pre_grad)


FIRST = (1, 7)
LANES = ((2, 3), (6, 5), (4, 8))


def on_device(inputs, encoder, enc_bias, active_blocks, near_decoders, far_decoders, targets):
    parts = lax.axis_size("width") // HALVES
    slots = near_decoders.shape[1]
    place = lax.axis_index("blk")[None].astype(jnp.int32)
    column = lax.axis_index("width") % parts
    local_in = inputs[0]
    near, far = near_decoders[0], far_decoders[0]
    columns = encoder.shape[2] // parts
    per_part = columns // FBLK
    blocks = lax.dynamic_slice_in_dim(active_blocks[0], column * per_part, per_part, 1)
    bias = lax.dynamic_slice_in_dim(enc_bias, column * columns, columns, 1)

    first = [near[o] for o in FIRST]
    first, rest, local_in = lax.optimization_barrier((first, near, local_in))
    moved = {o: shifted_down(slot, o) for o, slot in zip(FIRST, first)}
    parted = pre_parts(local_in, encoder[0], parts)
    parted, early = lax.optimization_barrier((parted, [moved[o] for o in FIRST]))
    moved.update(zip(FIRST, early))
    for lane in LANES:
        before = None
        for o in lane:
            slot = far if o == slots else rest[o]
            if before:
                slot, moved[before] = lax.optimization_barrier((slot, moved[before]))
            moved[o] = shifted_down(slot, o)
            before = o
    far_moved = moved[slots]

    acts = summed_over_width(parted, bias, blocks)
    moved = [moved[o] for o in range(1, slots)]
    shares = forward_shares(place, acts, near, moved, far, far_moved)
    own, other, sent = share_sums(place, exchange(shares, "blk"))
    reconstruction, own_grads = residual(
        place, own, other, other_half(sent), targets[0], other_half(targets[0])
    )
    all_grads = exchange(own_grads, "blk")
    grad_parts = backward_parts(place, all_grads, near, moved, far, far_moved, parts)
    pre_grad = summed_over_width(grad_parts, jnp.zeros_like(bias), blocks)
    enc_grad, bias_grad = encoder_grads(local_in, pre_grad)
    return reconstruction[None], enc_grad[None], bias_grad


def solution(mesh):
    return jax.shard_map(
        on_device,
        mesh=mesh,
        in_specs=(
            P("blk", None, "width"),
            P("blk", "width", None),
            P("blk", None),
            P("blk", None, None),
            P("blk", None, None, "width"),
            P("blk", None, "width"),
            P("blk", None, "width"),
        ),
        out_specs=(P("blk", None, "width"), P("blk", "width", None), P("blk", None)),
        check_vma=False,
    )
```

```python
import functools

import jax
import jax.numpy as jnp
from jax import lax
from jax.experimental import pallas as pl
from jax.experimental.pallas import tpu as pltpu
from jax.sharding import PartitionSpec as P

FBLK = 128
BF16 = jnp.bfloat16
F32 = jnp.float32
HALVES = 2
OPERANDS = (2, 6, 1, 3, 4, 5, 7, 8)
SMEM = pltpu.MemorySpace.SMEM
VMEM_LIMIT = 40 * 1024 * 1024


def exchange(parts, axis, runs=1):
    count = lax.axis_size(axis) // runs
    groups = [list(range(r * count, (r + 1) * count)) for r in range(runs)]
    return lax.all_to_all(parts, axis, 0, 0, tiled=True, axis_index_groups=groups)


def crossed(low, high, layers):
    spread = high - low
    half = layers // 2
    return (low < half) & (high >= half) & (low % 2 == 1) & (spread < half)


def shifted_down(block, distance):
    layers, parts = lax.axis_size("blk"), lax.axis_size("width")
    route = []
    for high in range(distance, layers):
        low = high - distance
        turn = parts // 2 if crossed(low, high, layers) else 0
        for part in range(parts):
            route.append((high * parts + part, low * parts + (part + turn) % parts))
    return lax.ppermute(block, ("blk", "width"), route)


def other_half(block):
    parts = lax.axis_size("width")
    return lax.ppermute(block, "width", [(p, (p + parts // 2) % parts) for p in range(parts)])


def pre_kernel(in_ref, enc_ref, out_ref):
    columns = out_ref.shape[2]
    product = jnp.dot(in_ref[...], enc_ref[...], preferred_element_type=F32)
    for part in range(out_ref.shape[0]):
        out_ref[part] = product[:, part * columns : (part + 1) * columns].astype(BF16)


def pre_parts(local_in, encoder, parts):
    tokens, rows = local_in.shape
    features = encoder.shape[1]
    columns = features // parts
    step = 2
    return pl.pallas_call(
        pre_kernel,
        grid=(parts // step,),
        in_specs=[
            pl.BlockSpec((tokens, rows), lambda c: (0, 0)),
            pl.BlockSpec((rows, step * columns), lambda c: (0, c)),
        ],
        out_specs=pl.BlockSpec((step, tokens, columns), lambda c: (c, 0, 0)),
        out_shape=jax.ShapeDtypeStruct((parts, tokens, columns), BF16),
        name="pre_parts",
    )(local_in, encoder)


def part_sum_kernel(parts_ref, out_ref):
    total = parts_ref[0].astype(F32)
    for part in range(1, parts_ref.shape[0]):
        total = total + parts_ref[part].astype(F32)
    out_ref[...] = total.astype(BF16)


def part_sum(parts):
    return pl.pallas_call(
        part_sum_kernel,
        out_shape=jax.ShapeDtypeStruct(parts.shape[1:], BF16),
        name="part_sum",
    )(parts)


def masked_sum_kernel(own_ref, came_ref, bias_ref, blocks_ref, out_ref):
    tokens, columns = own_ref.shape
    total = own_ref[...].astype(F32) + came_ref[...].astype(F32) + bias_ref[...]
    mask = spread_mask(blocks_ref[...])
    value = (mask * total).astype(BF16)
    for part in range(out_ref.shape[0]):
        out_ref[part] = value


def masked_sum(own, came, bias, blocks, parts):
    return pl.pallas_call(
        masked_sum_kernel,
        out_shape=jax.ShapeDtypeStruct((parts, *own.shape), BF16),
        name="masked_sum",
    )(own, came, bias, blocks)


def spread_mask(blocks):
    tokens, count = blocks.shape
    blocks = blocks.astype(F32)
    return jnp.concatenate(
        [jnp.broadcast_to(blocks[:, b : b + 1], (tokens, FBLK)) for b in range(count)], axis=1
    )


def masked_total_kernel(parts_ref, blocks_ref, out_ref):
    total = parts_ref[0].astype(F32)
    for part in range(1, parts_ref.shape[0]):
        total = total + parts_ref[part].astype(F32)
    value = (spread_mask(blocks_ref[...]) * total).astype(BF16)
    for part in range(out_ref.shape[0]):
        out_ref[part] = value


def masked_total(parts, blocks):
    return pl.pallas_call(
        masked_total_kernel,
        out_shape=jax.ShapeDtypeStruct(parts.shape, BF16),
        name="masked_total",
    )(parts, blocks)


def summed_over_width(parts, bias, blocks):
    own = part_sum(exchange(parts, "width", HALVES))
    return exchange(masked_sum(own, other_half(own), bias, blocks, parts.shape[0]), "width", HALVES)


def weight_specs(near_shape, far_shape, chunk):
    slots, features, cols = near_shape
    far_chunks = far_shape[0] // chunk
    whole = pl.BlockSpec((chunk, cols), lambda c, *_: (c, 0))
    lower = pl.BlockSpec((chunk, cols), lambda c, *_: (jnp.minimum(c, far_chunks - 1), 0))
    upper = pl.BlockSpec((chunk, cols), lambda c, *_: (jnp.maximum(c - far_chunks, 0), 0))
    near = pl.BlockSpec((slots, chunk, cols), lambda c, *_: (0, c, 0))
    return [near, lower] + [upper if o == slots else whole for o in OPERANDS]


def decoders_up(step, near_ref, far_ref, moved_refs, far_chunks):
    slots = near_ref.shape[0]
    moved = dict(zip(OPERANDS, moved_refs))
    found = [near_ref[0]] + [moved[o][...] for o in range(1, slots)]
    found.append(jnp.where(step < far_chunks, far_ref[...], moved[slots][...]))
    found += [near_ref[2 * slots - r] for r in range(slots + 1, 2 * slots)]
    return found


def forward_kernel(far_chunks, place_ref, acts_ref, near_ref, far_ref, *refs):
    slots = near_ref.shape[0]
    moved_refs, (out_ref, total_ref) = refs[:slots], refs[slots:]
    step = pl.program_id(0)
    layers = 2 * slots
    cols = near_ref.shape[2]

    @pl.when(step == 0)
    def _():
        total_ref[...] = jnp.zeros_like(total_ref)

    acts = jnp.concatenate([acts_ref[p] for p in range(acts_ref.shape[0])], axis=1)
    weights = decoders_up(step, near_ref, far_ref, moved_refs, far_chunks)
    for pair in range(slots):
        both = jnp.concatenate(weights[2 * pair : 2 * pair + 2], axis=1)
        total_ref[pair] += jnp.dot(acts, both, preferred_element_type=F32)

    @pl.when(step == pl.num_programs(0) - 1)
    def _():
        place = place_ref[0]
        for r in range(layers):
            share = total_ref[r // 2, :, (r % 2) * cols : (r % 2 + 1) * cols]
            kept = jnp.where(place + r < layers, share, 0.0)
            out_ref[lax.rem(place + r, layers)] = kept.astype(BF16)


def forward_shares(place, acts, near, far, moved, chunk=512):
    slots, features, cols = near.shape
    parts, tokens, columns = acts.shape
    layers = 2 * slots
    return pl.pallas_call(
        functools.partial(forward_kernel, far.shape[0] // chunk),
        grid=(features // chunk,),
        in_specs=[
            pl.BlockSpec(memory_space=SMEM),
            pl.BlockSpec((chunk // columns, tokens, columns), lambda c: (c, 0, 0)),
            *weight_specs(near.shape, far.shape, chunk),
        ],
        out_specs=pl.BlockSpec((layers, tokens, cols), lambda c: (0, 0, 0)),
        out_shape=jax.ShapeDtypeStruct((layers, tokens, cols), BF16),
        scratch_shapes=[pltpu.VMEM((slots, tokens, 2 * cols), F32)],
        compiler_params=pltpu.CompilerParams(vmem_limit_bytes=VMEM_LIMIT),
        name="forward_shares",
    )(place, acts, near, far, *moved)


def share_sums_kernel(place_ref, shares_ref, own_ref, other_ref, sent_ref):
    layers = shares_ref.shape[0]
    place = place_ref[0]
    own = jnp.zeros(own_ref.shape, F32)
    other = jnp.zeros(own_ref.shape, F32)
    for low in range(layers):
        share = shares_ref[low].astype(F32)
        away = crossed(low, place, layers)
        own = own + jnp.where(away, 0.0, share)
        other = other + jnp.where(away, share, 0.0)
    own_ref[...] = own
    other_ref[...] = other
    sent_ref[0] = own.astype(BF16)
    sent_ref[1] = other.astype(BF16)


def share_sums(place, shares):
    _, tokens, cols = shares.shape
    return pl.pallas_call(
        share_sums_kernel,
        in_specs=[pl.BlockSpec(memory_space=SMEM), pl.BlockSpec(memory_space=pltpu.VMEM)],
        out_shape=(
            jax.ShapeDtypeStruct((tokens, cols), F32),
            jax.ShapeDtypeStruct((tokens, cols), F32),
            jax.ShapeDtypeStruct((2, tokens, cols), BF16),
        ),
        name="share_sums",
    )(place, shares)


def residual_kernel(place_ref, own_ref, other_ref, came_ref, target_ref, away_target_ref, rec_ref, grads_ref):
    layers = grads_ref.shape[0]
    place = place_ref[0]
    rec = own_ref[...] + came_ref[1].astype(F32)
    away_rec = other_ref[...] + came_ref[0].astype(F32)
    rec_ref[...] = rec
    grad = (rec - target_ref[...].astype(F32)).astype(BF16)
    away_grad = (away_rec - away_target_ref[...].astype(F32)).astype(BF16)
    for low in range(layers):
        grads_ref[low] = jnp.where(crossed(low, place, layers), away_grad, grad)


def residual(place, own, other, came, target, away_target):
    layers = lax.axis_size("blk")
    vmem = pl.BlockSpec(memory_space=pltpu.VMEM)
    return pl.pallas_call(
        residual_kernel,
        in_specs=[pl.BlockSpec(memory_space=SMEM)] + [vmem] * 5,
        out_shape=(
            jax.ShapeDtypeStruct(target.shape, F32),
            jax.ShapeDtypeStruct((layers, *target.shape), BF16),
        ),
        name="residual",
    )(place, own, other, came, target, away_target)


def backward_kernel(far_chunks, place_ref, grads_ref, near_ref, far_ref, *refs):
    slots = near_ref.shape[0]
    moved_refs, (out_ref, up_ref) = refs[:slots], refs[slots:]
    step = pl.program_id(0)
    layers = 2 * slots
    cols = near_ref.shape[2]
    columns = out_ref.shape[2]

    @pl.when(step == 0)
    def _():
        place = place_ref[0]
        for r in range(layers):
            grad = grads_ref[lax.rem(place + r, layers)]
            up_ref[:, r * cols : (r + 1) * cols] = jnp.where(
                place + r < layers, grad, jnp.zeros_like(grad)
            )

    weights = decoders_up(step, near_ref, far_ref, moved_refs, far_chunks)
    product = lax.dot_general(
        up_ref[...],
        jnp.concatenate(weights, axis=1),
        (((1,), (1,)), ((), ())),
        preferred_element_type=F32,
    )
    for part in range(out_ref.shape[0]):
        out_ref[part] = product[:, part * columns : (part + 1) * columns].astype(BF16)


def backward_parts(place, grads, near, far, moved, parts, chunk=512):
    slots, features, cols = near.shape
    layers, tokens, _ = grads.shape
    columns = features // parts
    return pl.pallas_call(
        functools.partial(backward_kernel, far.shape[0] // chunk),
        grid=(features // chunk,),
        in_specs=[
            pl.BlockSpec(memory_space=SMEM),
            pl.BlockSpec(grads.shape, lambda c: (0, 0, 0)),
            *weight_specs(near.shape, far.shape, chunk),
        ],
        out_specs=pl.BlockSpec((chunk // columns, tokens, columns), lambda c: (c, 0, 0)),
        out_shape=jax.ShapeDtypeStruct((parts, tokens, columns), BF16),
        scratch_shapes=[pltpu.VMEM((tokens, layers * cols), BF16)],
        compiler_params=pltpu.CompilerParams(vmem_limit_bytes=VMEM_LIMIT),
        name="backward_parts",
    )(place, grads, near, far, *moved)


def encoder_grad_kernel(in_ref, pre_ref, enc_ref, bias_ref):
    columns = pre_ref.shape[2]
    for part in range(pre_ref.shape[0]):
        grad = pre_ref[part]
        span = slice(part * columns, (part + 1) * columns)
        enc_ref[:, span] = lax.dot_general(
            in_ref[...], grad, (((0,), (0,)), ((), ())), preferred_element_type=F32
        ).astype(BF16)
        bias_ref[:, span] = jnp.sum(grad.astype(F32), axis=0, keepdims=True)


def encoder_grads(local_in, pre_grad):
    tokens, rows = local_in.shape
    parts, _, columns = pre_grad.shape
    step = 4
    return pl.pallas_call(
        encoder_grad_kernel,
        grid=(parts // step,),
        in_specs=[
            pl.BlockSpec((tokens, rows), lambda c: (0, 0)),
            pl.BlockSpec((step, tokens, columns), lambda c: (c, 0, 0)),
        ],
        out_specs=[
            pl.BlockSpec((rows, step * columns), lambda c: (0, c)),
            pl.BlockSpec((1, step * columns), lambda c: (0, c)),
        ],
        out_shape=(
            jax.ShapeDtypeStruct((rows, parts * columns), BF16),
            jax.ShapeDtypeStruct((1, parts * columns), F32),
        ),
        name="encoder_grads",
    )(local_in, pre_grad)


TARGET = 0
LANES = ((4, 2), (3, 6), (5, 1), (7, 8, 0))


def on_device(inputs, encoder, enc_bias, active_blocks, near_decoders, far_decoders, targets):
    parts = lax.axis_size("width") // HALVES
    slots = near_decoders.shape[1]
    place = lax.axis_index("blk")[None].astype(jnp.int32)
    column = lax.axis_index("width") % parts
    local_in = inputs[0]
    near, far = near_decoders[0], far_decoders[0]
    columns = encoder.shape[2] // parts
    per_part = columns // FBLK
    blocks = lax.dynamic_slice_in_dim(active_blocks[0], column * per_part, per_part, 1)
    bias = lax.dynamic_slice_in_dim(enc_bias, column * columns, columns, 1)

    first = [near[lane[0]] for lane in LANES]
    first, rest, local_in = lax.optimization_barrier((first, near, local_in))
    moved = {}
    away_target = targets[0]
    for lane, slot in zip(LANES, first):
        before = None
        for o in lane:
            if before is None:
                moved[o] = shifted_down(slot, o)
            elif o == TARGET:
                away_target, moved[before] = lax.optimization_barrier((away_target, moved[before]))
                away_target = other_half(away_target)
            else:
                slot, moved[before] = lax.optimization_barrier(
                    (far if o == slots else rest[o], moved[before])
                )
                moved[o] = shifted_down(slot, o)
            before = o
    parted = pre_parts(local_in, encoder[0], parts)

    acts = summed_over_width(parted, bias, blocks)
    moved = [moved[o] for o in OPERANDS]
    shares = forward_shares(place, acts, near, far, moved)
    shares, away_target = lax.optimization_barrier((shares, away_target))
    own, other, sent = share_sums(place, exchange(shares, "blk"))
    reconstruction, own_grads = residual(
        place, own, other, other_half(sent), targets[0], away_target
    )
    all_grads = exchange(own_grads, "blk")
    all_parts = lax.axis_size("width")
    grad_parts = backward_parts(place, all_grads, near, far, moved, all_parts)
    few = active_blocks.shape[2] // all_parts
    own_blocks = lax.dynamic_slice_in_dim(
        active_blocks[0], lax.axis_index("width") * few, few, 1
    )
    pre_part = masked_total(exchange(grad_parts, "width"), own_blocks)
    pre_grad = exchange(pre_part, "width")
    enc_grad, bias_grad = encoder_grads(local_in, pre_grad)
    return reconstruction[None], enc_grad[None], bias_grad


def solution(mesh):
    return jax.shard_map(
        on_device,
        mesh=mesh,
        in_specs=(
            P("blk", None, "width"),
            P("blk", "width", None),
            P("blk", None),
            P("blk", None, None),
            P("blk", None, None, "width"),
            P("blk", None, "width"),
            P("blk", None, "width"),
        ),
        out_specs=(P("blk", None, "width"), P("blk", "width", None), P("blk", None)),
        check_vma=False,
    )
```

```python
import functools

import jax
import jax.numpy as jnp
from jax import lax
from jax.experimental import pallas as pl
from jax.experimental.pallas import tpu as pltpu
from jax.sharding import PartitionSpec as P

FBLK = 128
BF16 = jnp.bfloat16
F32 = jnp.float32
HALVES = 2
OPERANDS = (2, 6, 1, 3, 4, 5, 7, 8)
SMEM = pltpu.MemorySpace.SMEM
VMEM_LIMIT = 40 * 1024 * 1024


def exchange(parts, axis, runs=1):
    count = lax.axis_size(axis) // runs
    groups = [list(range(r * count, (r + 1) * count)) for r in range(runs)]
    return lax.all_to_all(parts, axis, 0, 0, tiled=True, axis_index_groups=groups)


def crossed(low, high, layers):
    spread = high - low
    half = layers // 2
    return (low < half) & (high >= half) & (low % 2 == 1) & (spread < half)


def shifted_down(block, distance):
    layers, parts = lax.axis_size("blk"), lax.axis_size("width")
    route = []
    for high in range(distance, layers):
        low = high - distance
        turn = parts // 2 if crossed(low, high, layers) else 0
        for part in range(parts):
            route.append((high * parts + part, low * parts + (part + turn) % parts))
    return lax.ppermute(block, ("blk", "width"), route)


def other_half(block):
    parts = lax.axis_size("width")
    return lax.ppermute(block, "width", [(p, (p + parts // 2) % parts) for p in range(parts)])


def pre_kernel(in_ref, enc_ref, out_ref):
    columns = out_ref.shape[2]
    product = jnp.dot(in_ref[...], enc_ref[...], preferred_element_type=F32)
    for part in range(out_ref.shape[0]):
        out_ref[part] = product[:, part * columns : (part + 1) * columns].astype(BF16)


def pre_parts(local_in, encoder, parts):
    tokens, rows = local_in.shape
    features = encoder.shape[1]
    columns = features // parts
    step = 2
    return pl.pallas_call(
        pre_kernel,
        grid=(parts // step,),
        in_specs=[
            pl.BlockSpec((tokens, rows), lambda c: (0, 0)),
            pl.BlockSpec((rows, step * columns), lambda c: (0, c)),
        ],
        out_specs=pl.BlockSpec((step, tokens, columns), lambda c: (c, 0, 0)),
        out_shape=jax.ShapeDtypeStruct((parts, tokens, columns), BF16),
        name="pre_parts",
    )(local_in, encoder)


def part_sum_kernel(parts_ref, out_ref):
    total = parts_ref[0].astype(F32)
    for part in range(1, parts_ref.shape[0]):
        total = total + parts_ref[part].astype(F32)
    out_ref[...] = total.astype(BF16)


def part_sum(parts):
    return pl.pallas_call(
        part_sum_kernel,
        out_shape=jax.ShapeDtypeStruct(parts.shape[1:], BF16),
        name="part_sum",
    )(parts)


def masked_sum_kernel(own_ref, came_ref, bias_ref, blocks_ref, out_ref):
    tokens, columns = own_ref.shape
    total = own_ref[...].astype(F32) + came_ref[...].astype(F32) + bias_ref[...]
    mask = spread_mask(blocks_ref[...])
    value = (mask * total).astype(BF16)
    for part in range(out_ref.shape[0]):
        out_ref[part] = value


def masked_sum(own, came, bias, blocks, parts):
    return pl.pallas_call(
        masked_sum_kernel,
        out_shape=jax.ShapeDtypeStruct((parts, *own.shape), BF16),
        name="masked_sum",
    )(own, came, bias, blocks)


def spread_mask(blocks):
    tokens, count = blocks.shape
    blocks = blocks.astype(F32)
    return jnp.concatenate(
        [jnp.broadcast_to(blocks[:, b : b + 1], (tokens, FBLK)) for b in range(count)], axis=1
    )


def masked_total_kernel(parts_ref, blocks_ref, out_ref):
    total = parts_ref[0].astype(F32)
    for part in range(1, parts_ref.shape[0]):
        total = total + parts_ref[part].astype(F32)
    value = (spread_mask(blocks_ref[...]) * total).astype(BF16)
    for part in range(out_ref.shape[0]):
        out_ref[part] = value


def masked_total(parts, blocks):
    return pl.pallas_call(
        masked_total_kernel,
        out_shape=jax.ShapeDtypeStruct(parts.shape, BF16),
        name="masked_total",
    )(parts, blocks)


def summed_over_width(parts, bias, blocks):
    own = part_sum(exchange(parts, "width", HALVES))
    return exchange(masked_sum(own, other_half(own), bias, blocks, parts.shape[0]), "width", HALVES)


def weight_specs(near_shape, far_shape, chunk):
    slots, features, cols = near_shape
    far_chunks = far_shape[0] // chunk
    whole = pl.BlockSpec((chunk, cols), lambda c, *_: (c, 0))
    lower = pl.BlockSpec((chunk, cols), lambda c, *_: (jnp.minimum(c, far_chunks - 1), 0))
    upper = pl.BlockSpec((chunk, cols), lambda c, *_: (jnp.maximum(c - far_chunks, 0), 0))
    near = pl.BlockSpec((slots, chunk, cols), lambda c, *_: (0, c, 0))
    return [near, lower] + [upper if o == slots else whole for o in OPERANDS]


def decoders_up(step, near_ref, far_ref, moved_refs, far_chunks):
    slots = near_ref.shape[0]
    moved = dict(zip(OPERANDS, moved_refs))
    found = [near_ref[0]] + [moved[o][...] for o in range(1, slots)]
    found.append(jnp.where(step < far_chunks, far_ref[...], moved[slots][...]))
    found += [near_ref[2 * slots - r] for r in range(slots + 1, 2 * slots)]
    return found


def forward_kernel(far_chunks, place_ref, acts_ref, near_ref, far_ref, *refs):
    slots = near_ref.shape[0]
    moved_refs, (out_ref, total_ref) = refs[:slots], refs[slots:]
    step = pl.program_id(0)
    layers = 2 * slots
    cols = near_ref.shape[2]

    @pl.when(step == 0)
    def _():
        total_ref[...] = jnp.zeros_like(total_ref)

    acts = jnp.concatenate([acts_ref[p] for p in range(acts_ref.shape[0])], axis=1)
    weights = decoders_up(step, near_ref, far_ref, moved_refs, far_chunks)
    for pair in range(slots):
        both = jnp.concatenate(weights[2 * pair : 2 * pair + 2], axis=1)
        total_ref[pair] += jnp.dot(acts, both, preferred_element_type=F32)

    @pl.when(step == pl.num_programs(0) - 1)
    def _():
        place = place_ref[0]
        for r in range(layers):
            share = total_ref[r // 2, :, (r % 2) * cols : (r % 2 + 1) * cols]
            kept = jnp.where(place + r < layers, share, 0.0)
            out_ref[lax.rem(place + r, layers)] = kept.astype(BF16)


def forward_shares(place, acts, near, far, moved, chunk=1024):
    slots, features, cols = near.shape
    parts, tokens, columns = acts.shape
    layers = 2 * slots
    return pl.pallas_call(
        functools.partial(forward_kernel, far.shape[0] // chunk),
        grid=(features // chunk,),
        in_specs=[
            pl.BlockSpec(memory_space=SMEM),
            pl.BlockSpec((chunk // columns, tokens, columns), lambda c: (c, 0, 0)),
            *weight_specs(near.shape, far.shape, chunk),
        ],
        out_specs=pl.BlockSpec((layers, tokens, cols), lambda c: (0, 0, 0)),
        out_shape=jax.ShapeDtypeStruct((layers, tokens, cols), BF16),
        scratch_shapes=[pltpu.VMEM((slots, tokens, 2 * cols), F32)],
        compiler_params=pltpu.CompilerParams(vmem_limit_bytes=VMEM_LIMIT),
        name="forward_shares",
    )(place, acts, near, far, *moved)


def share_sums_kernel(place_ref, shares_ref, own_ref, other_ref, sent_ref):
    layers = shares_ref.shape[0]
    place = place_ref[0]
    own = jnp.zeros(own_ref.shape, F32)
    other = jnp.zeros(own_ref.shape, F32)
    for low in range(layers):
        share = shares_ref[low].astype(F32)
        away = crossed(low, place, layers)
        own = own + jnp.where(away, 0.0, share)
        other = other + jnp.where(away, share, 0.0)
    own_ref[...] = own
    other_ref[...] = other
    sent_ref[0] = own.astype(BF16)
    sent_ref[1] = other.astype(BF16)


def share_sums(place, shares):
    _, tokens, cols = shares.shape
    return pl.pallas_call(
        share_sums_kernel,
        in_specs=[pl.BlockSpec(memory_space=SMEM), pl.BlockSpec(memory_space=pltpu.VMEM)],
        out_shape=(
            jax.ShapeDtypeStruct((tokens, cols), F32),
            jax.ShapeDtypeStruct((tokens, cols), F32),
            jax.ShapeDtypeStruct((2, tokens, cols), BF16),
        ),
        name="share_sums",
    )(place, shares)


def residual_kernel(place_ref, own_ref, other_ref, came_ref, target_ref, away_target_ref, rec_ref, grads_ref):
    layers = grads_ref.shape[0]
    place = place_ref[0]
    rec = own_ref[...] + came_ref[1].astype(F32)
    away_rec = other_ref[...] + came_ref[0].astype(F32)
    rec_ref[...] = rec
    grad = (rec - target_ref[...].astype(F32)).astype(BF16)
    away_grad = (away_rec - away_target_ref[...].astype(F32)).astype(BF16)
    for low in range(layers):
        grads_ref[low] = jnp.where(crossed(low, place, layers), away_grad, grad)


def residual(place, own, other, came, target, away_target):
    layers = lax.axis_size("blk")
    vmem = pl.BlockSpec(memory_space=pltpu.VMEM)
    return pl.pallas_call(
        residual_kernel,
        in_specs=[pl.BlockSpec(memory_space=SMEM)] + [vmem] * 5,
        out_shape=(
            jax.ShapeDtypeStruct(target.shape, F32),
            jax.ShapeDtypeStruct((layers, *target.shape), BF16),
        ),
        name="residual",
    )(place, own, other, came, target, away_target)


def backward_kernel(far_chunks, place_ref, grads_ref, near_ref, far_ref, *refs):
    slots = near_ref.shape[0]
    moved_refs, (out_ref, up_ref) = refs[:slots], refs[slots:]
    step = pl.program_id(0)
    layers = 2 * slots
    cols = near_ref.shape[2]
    columns = out_ref.shape[2]

    @pl.when(step == 0)
    def _():
        place = place_ref[0]
        for r in range(layers):
            grad = grads_ref[lax.rem(place + r, layers)]
            up_ref[:, r * cols : (r + 1) * cols] = jnp.where(
                place + r < layers, grad, jnp.zeros_like(grad)
            )

    weights = decoders_up(step, near_ref, far_ref, moved_refs, far_chunks)
    product = lax.dot_general(
        up_ref[...],
        jnp.concatenate(weights, axis=1),
        (((1,), (1,)), ((), ())),
        preferred_element_type=F32,
    )
    for part in range(out_ref.shape[0]):
        out_ref[part] = product[:, part * columns : (part + 1) * columns].astype(BF16)


def backward_parts(place, grads, near, far, moved, parts, chunk=1024):
    slots, features, cols = near.shape
    layers, tokens, _ = grads.shape
    columns = features // parts
    return pl.pallas_call(
        functools.partial(backward_kernel, far.shape[0] // chunk),
        grid=(features // chunk,),
        in_specs=[
            pl.BlockSpec(memory_space=SMEM),
            pl.BlockSpec(grads.shape, lambda c: (0, 0, 0)),
            *weight_specs(near.shape, far.shape, chunk),
        ],
        out_specs=pl.BlockSpec((chunk // columns, tokens, columns), lambda c: (c, 0, 0)),
        out_shape=jax.ShapeDtypeStruct((parts, tokens, columns), BF16),
        scratch_shapes=[pltpu.VMEM((tokens, layers * cols), BF16)],
        compiler_params=pltpu.CompilerParams(vmem_limit_bytes=VMEM_LIMIT),
        name="backward_parts",
    )(place, grads, near, far, *moved)


def encoder_grad_kernel(in_ref, pre_ref, enc_ref, bias_ref):
    columns = pre_ref.shape[2]
    for part in range(pre_ref.shape[0]):
        grad = pre_ref[part]
        span = slice(part * columns, (part + 1) * columns)
        enc_ref[:, span] = lax.dot_general(
            in_ref[...], grad, (((0,), (0,)), ((), ())), preferred_element_type=F32
        ).astype(BF16)
        bias_ref[:, span] = jnp.sum(grad.astype(F32), axis=0, keepdims=True)


def encoder_grads(local_in, pre_grad):
    tokens, rows = local_in.shape
    parts, _, columns = pre_grad.shape
    step = 8
    return pl.pallas_call(
        encoder_grad_kernel,
        grid=(parts // step,),
        in_specs=[
            pl.BlockSpec((tokens, rows), lambda c: (0, 0)),
            pl.BlockSpec((step, tokens, columns), lambda c: (c, 0, 0)),
        ],
        out_specs=[
            pl.BlockSpec((rows, step * columns), lambda c: (0, c)),
            pl.BlockSpec((1, step * columns), lambda c: (0, c)),
        ],
        out_shape=(
            jax.ShapeDtypeStruct((rows, parts * columns), BF16),
            jax.ShapeDtypeStruct((1, parts * columns), F32),
        ),
        name="encoder_grads",
    )(local_in, pre_grad)


TARGET = 0
LANES = ((4, 2), (3, 6), (5, 1), (7, 8, 0))


def on_device(inputs, encoder, enc_bias, active_blocks, near_decoders, far_decoders, targets):
    parts = lax.axis_size("width") // HALVES
    slots = near_decoders.shape[1]
    place = lax.axis_index("blk")[None].astype(jnp.int32)
    column = lax.axis_index("width") % parts
    local_in = inputs[0]
    near, far = near_decoders[0], far_decoders[0]
    columns = encoder.shape[2] // parts
    per_part = columns // FBLK
    blocks = lax.dynamic_slice_in_dim(active_blocks[0], column * per_part, per_part, 1)
    bias = lax.dynamic_slice_in_dim(enc_bias, column * columns, columns, 1)

    first = [near[lane[0]] for lane in LANES]
    first, rest = lax.optimization_barrier((first, near))
    moved = {}
    away_target = targets[0]
    for lane, slot in zip(LANES, first):
        before = None
        for o in lane:
            if before is None:
                moved[o] = shifted_down(slot, o)
            elif o == TARGET:
                away_target, moved[before] = lax.optimization_barrier((away_target, moved[before]))
                away_target = other_half(away_target)
            else:
                slot, moved[before] = lax.optimization_barrier(
                    (far if o == slots else rest[o], moved[before])
                )
                moved[o] = shifted_down(slot, o)
            before = o
    parted = pre_parts(local_in, encoder[0], parts)

    acts = summed_over_width(parted, bias, blocks)
    moved = [moved[o] for o in OPERANDS]
    shares = forward_shares(place, acts, near, far, moved)
    shares, away_target = lax.optimization_barrier((shares, away_target))
    own, other, sent = share_sums(place, exchange(shares, "blk"))
    reconstruction, own_grads = residual(
        place, own, other, other_half(sent), targets[0], away_target
    )
    all_grads = exchange(own_grads, "blk")
    all_parts = lax.axis_size("width")
    grad_parts = backward_parts(place, all_grads, near, far, moved, all_parts)
    few = active_blocks.shape[2] // all_parts
    own_blocks = lax.dynamic_slice_in_dim(
        active_blocks[0], lax.axis_index("width") * few, few, 1
    )
    pre_part = masked_total(exchange(grad_parts, "width"), own_blocks)
    pre_grad = exchange(pre_part, "width")
    enc_grad, bias_grad = encoder_grads(local_in, pre_grad)
    return reconstruction[None], enc_grad[None], bias_grad


def solution(mesh):
    return jax.shard_map(
        on_device,
        mesh=mesh,
        in_specs=(
            P("blk", None, "width"),
            P("blk", "width", None),
            P("blk", None),
            P("blk", None, None),
            P("blk", None, None, "width"),
            P("blk", None, "width"),
            P("blk", None, "width"),
        ),
        out_specs=(P("blk", None, "width"), P("blk", "width", None), P("blk", None)),
        check_vma=False,
    )
```

```python
import functools

import jax
import jax.numpy as jnp
from jax import lax
from jax.experimental import pallas as pl
from jax.experimental.pallas import tpu as pltpu
from jax.sharding import PartitionSpec as P

FBLK = 128
BF16 = jnp.bfloat16
F32 = jnp.float32
HALVES = 2
OPERANDS = (2, 6, 1, 3, 4, 5, 7, 8)
SMEM = pltpu.MemorySpace.SMEM
VMEM_LIMIT = 40 * 1024 * 1024


def exchange(parts, axis, runs=1):
    count = lax.axis_size(axis) // runs
    groups = [list(range(r * count, (r + 1) * count)) for r in range(runs)]
    return lax.all_to_all(parts, axis, 0, 0, tiled=True, axis_index_groups=groups)


def crossed(low, high, layers):
    spread = high - low
    half = layers // 2
    return (low < half) & (high >= half) & (low % 2 == 1) & (spread < half)


def shifted_down(block, distance):
    layers, parts = lax.axis_size("blk"), lax.axis_size("width")
    route = []
    for high in range(distance, layers):
        low = high - distance
        turn = parts // 2 if crossed(low, high, layers) else 0
        for part in range(parts):
            route.append((high * parts + part, low * parts + (part + turn) % parts))
    return lax.ppermute(block, ("blk", "width"), route)


def other_half(block):
    parts = lax.axis_size("width")
    return lax.ppermute(block, "width", [(p, (p + parts // 2) % parts) for p in range(parts)])


def pre_kernel(in_ref, enc_ref, out_ref):
    columns = out_ref.shape[2]
    product = jnp.dot(in_ref[...], enc_ref[...], preferred_element_type=F32)
    for part in range(out_ref.shape[0]):
        out_ref[part] = product[:, part * columns : (part + 1) * columns].astype(BF16)


def pre_parts(local_in, encoder, parts):
    tokens, rows = local_in.shape
    features = encoder.shape[1]
    columns = features // parts
    step = 2
    return pl.pallas_call(
        pre_kernel,
        grid=(parts // step,),
        in_specs=[
            pl.BlockSpec((tokens, rows), lambda c: (0, 0)),
            pl.BlockSpec((rows, step * columns), lambda c: (0, c)),
        ],
        out_specs=pl.BlockSpec((step, tokens, columns), lambda c: (c, 0, 0)),
        out_shape=jax.ShapeDtypeStruct((parts, tokens, columns), BF16),
        name="pre_parts",
    )(local_in, encoder)


def part_sum_kernel(parts_ref, out_ref):
    total = parts_ref[0].astype(F32)
    for part in range(1, parts_ref.shape[0]):
        total = total + parts_ref[part].astype(F32)
    out_ref[...] = total.astype(BF16)


def part_sum(parts):
    return pl.pallas_call(
        part_sum_kernel,
        out_shape=jax.ShapeDtypeStruct(parts.shape[1:], BF16),
        name="part_sum",
    )(parts)


def masked_sum_kernel(own_ref, came_ref, bias_ref, blocks_ref, out_ref):
    tokens, columns = own_ref.shape
    total = own_ref[...].astype(F32) + came_ref[...].astype(F32) + bias_ref[...]
    mask = spread_mask(blocks_ref[...])
    value = (mask * total).astype(BF16)
    for part in range(out_ref.shape[0]):
        out_ref[part] = value


def masked_sum(own, came, bias, blocks, parts):
    return pl.pallas_call(
        masked_sum_kernel,
        out_shape=jax.ShapeDtypeStruct((parts, *own.shape), BF16),
        name="masked_sum",
    )(own, came, bias, blocks)


def spread_mask(blocks):
    tokens, count = blocks.shape
    blocks = blocks.astype(F32)
    return jnp.concatenate(
        [jnp.broadcast_to(blocks[:, b : b + 1], (tokens, FBLK)) for b in range(count)], axis=1
    )


def masked_total_kernel(parts_ref, blocks_ref, out_ref):
    total = parts_ref[0].astype(F32)
    for part in range(1, parts_ref.shape[0]):
        total = total + parts_ref[part].astype(F32)
    value = (spread_mask(blocks_ref[...]) * total).astype(BF16)
    for part in range(out_ref.shape[0]):
        out_ref[part] = value


def masked_total(parts, blocks):
    return pl.pallas_call(
        masked_total_kernel,
        out_shape=jax.ShapeDtypeStruct(parts.shape, BF16),
        name="masked_total",
    )(parts, blocks)


def summed_over_width(parts, bias, blocks):
    own = part_sum(exchange(parts, "width", HALVES))
    return exchange(masked_sum(own, other_half(own), bias, blocks, parts.shape[0]), "width", HALVES)


def weight_specs(near_shape, far_shape, chunk):
    slots, features, cols = near_shape
    far_chunks = far_shape[0] // chunk
    whole = pl.BlockSpec((chunk, cols), lambda c, *_: (c, 0))
    lower = pl.BlockSpec((chunk, cols), lambda c, *_: (jnp.minimum(c, far_chunks - 1), 0))
    upper = pl.BlockSpec((chunk, cols), lambda c, *_: (jnp.maximum(c - far_chunks, 0), 0))
    near = pl.BlockSpec((slots, chunk, cols), lambda c, *_: (0, c, 0))
    return [near, lower] + [upper if o == slots else whole for o in OPERANDS]


def decoders_up(step, near_ref, far_ref, moved_refs, far_chunks):
    slots = near_ref.shape[0]
    moved = dict(zip(OPERANDS, moved_refs))
    found = [near_ref[0]] + [moved[o][...] for o in range(1, slots)]
    found.append(jnp.where(step < far_chunks, far_ref[...], moved[slots][...]))
    found += [near_ref[2 * slots - r] for r in range(slots + 1, 2 * slots)]
    return found


def forward_kernel(far_chunks, place_ref, acts_ref, near_ref, far_ref, *refs):
    slots = near_ref.shape[0]
    moved_refs, (out_ref, total_ref) = refs[:slots], refs[slots:]
    step = pl.program_id(0)
    layers = 2 * slots
    cols = near_ref.shape[2]

    @pl.when(step == 0)
    def _():
        total_ref[...] = jnp.zeros_like(total_ref)

    acts = jnp.concatenate([acts_ref[p] for p in range(acts_ref.shape[0])], axis=1)
    weights = decoders_up(step, near_ref, far_ref, moved_refs, far_chunks)
    for pair in range(slots):
        both = jnp.concatenate(weights[2 * pair : 2 * pair + 2], axis=1)
        total_ref[pair] += jnp.dot(acts, both, preferred_element_type=F32)

    @pl.when(step == pl.num_programs(0) - 1)
    def _():
        place = place_ref[0]
        for r in range(layers):
            share = total_ref[r // 2, :, (r % 2) * cols : (r % 2 + 1) * cols]
            kept = jnp.where(place + r < layers, share, 0.0)
            out_ref[lax.rem(place + r, layers)] = kept.astype(BF16)


def forward_shares(place, acts, near, far, moved, chunk=2048):
    slots, features, cols = near.shape
    parts, tokens, columns = acts.shape
    layers = 2 * slots
    return pl.pallas_call(
        functools.partial(forward_kernel, far.shape[0] // chunk),
        grid=(features // chunk,),
        in_specs=[
            pl.BlockSpec(memory_space=SMEM),
            pl.BlockSpec((chunk // columns, tokens, columns), lambda c: (c, 0, 0)),
            *weight_specs(near.shape, far.shape, chunk),
        ],
        out_specs=pl.BlockSpec((layers, tokens, cols), lambda c: (0, 0, 0)),
        out_shape=jax.ShapeDtypeStruct((layers, tokens, cols), BF16),
        scratch_shapes=[pltpu.VMEM((slots, tokens, 2 * cols), F32)],
        compiler_params=pltpu.CompilerParams(vmem_limit_bytes=VMEM_LIMIT),
        name="forward_shares",
    )(place, acts, near, far, *moved)


def share_sums_kernel(place_ref, shares_ref, own_ref, other_ref, sent_ref):
    layers = shares_ref.shape[0]
    place = place_ref[0]
    own = jnp.zeros(own_ref.shape, F32)
    other = jnp.zeros(own_ref.shape, F32)
    for low in range(layers):
        share = shares_ref[low].astype(F32)
        away = crossed(low, place, layers)
        own = own + jnp.where(away, 0.0, share)
        other = other + jnp.where(away, share, 0.0)
    own_ref[...] = own
    other_ref[...] = other
    sent_ref[0] = own.astype(BF16)
    sent_ref[1] = other.astype(BF16)


def share_sums(place, shares):
    _, tokens, cols = shares.shape
    return pl.pallas_call(
        share_sums_kernel,
        in_specs=[pl.BlockSpec(memory_space=SMEM), pl.BlockSpec(memory_space=pltpu.VMEM)],
        out_shape=(
            jax.ShapeDtypeStruct((tokens, cols), F32),
            jax.ShapeDtypeStruct((tokens, cols), F32),
            jax.ShapeDtypeStruct((2, tokens, cols), BF16),
        ),
        name="share_sums",
    )(place, shares)


def residual_kernel(place_ref, own_ref, other_ref, came_ref, target_ref, away_target_ref, rec_ref, grads_ref):
    layers = grads_ref.shape[0]
    place = place_ref[0]
    rec = own_ref[...] + came_ref[1].astype(F32)
    away_rec = other_ref[...] + came_ref[0].astype(F32)
    rec_ref[...] = rec
    grad = (rec - target_ref[...].astype(F32)).astype(BF16)
    away_grad = (away_rec - away_target_ref[...].astype(F32)).astype(BF16)
    for low in range(layers):
        grads_ref[low] = jnp.where(crossed(low, place, layers), away_grad, grad)


def residual(place, own, other, came, target, away_target):
    layers = lax.axis_size("blk")
    vmem = pl.BlockSpec(memory_space=pltpu.VMEM)
    return pl.pallas_call(
        residual_kernel,
        in_specs=[pl.BlockSpec(memory_space=SMEM)] + [vmem] * 5,
        out_shape=(
            jax.ShapeDtypeStruct(target.shape, F32),
            jax.ShapeDtypeStruct((layers, *target.shape), BF16),
        ),
        name="residual",
    )(place, own, other, came, target, away_target)


def backward_kernel(far_chunks, place_ref, grads_ref, near_ref, far_ref, *refs):
    slots = near_ref.shape[0]
    moved_refs, (out_ref, up_ref) = refs[:slots], refs[slots:]
    step = pl.program_id(0)
    layers = 2 * slots
    cols = near_ref.shape[2]
    columns = out_ref.shape[2]

    @pl.when(step == 0)
    def _():
        place = place_ref[0]
        for r in range(layers):
            grad = grads_ref[lax.rem(place + r, layers)]
            up_ref[:, r * cols : (r + 1) * cols] = jnp.where(
                place + r < layers, grad, jnp.zeros_like(grad)
            )

    weights = decoders_up(step, near_ref, far_ref, moved_refs, far_chunks)
    product = lax.dot_general(
        up_ref[...],
        jnp.concatenate(weights, axis=1),
        (((1,), (1,)), ((), ())),
        preferred_element_type=F32,
    )
    for part in range(out_ref.shape[0]):
        out_ref[part] = product[:, part * columns : (part + 1) * columns].astype(BF16)


def backward_parts(place, grads, near, far, moved, parts, chunk=2048):
    slots, features, cols = near.shape
    layers, tokens, _ = grads.shape
    columns = features // parts
    return pl.pallas_call(
        functools.partial(backward_kernel, far.shape[0] // chunk),
        grid=(features // chunk,),
        in_specs=[
            pl.BlockSpec(memory_space=SMEM),
            pl.BlockSpec(grads.shape, lambda c: (0, 0, 0)),
            *weight_specs(near.shape, far.shape, chunk),
        ],
        out_specs=pl.BlockSpec((chunk // columns, tokens, columns), lambda c: (c, 0, 0)),
        out_shape=jax.ShapeDtypeStruct((parts, tokens, columns), BF16),
        scratch_shapes=[pltpu.VMEM((tokens, layers * cols), BF16)],
        compiler_params=pltpu.CompilerParams(vmem_limit_bytes=VMEM_LIMIT),
        name="backward_parts",
    )(place, grads, near, far, *moved)


def encoder_grad_kernel(in_ref, pre_ref, enc_ref, bias_ref):
    columns = pre_ref.shape[2]
    for part in range(pre_ref.shape[0]):
        grad = pre_ref[part]
        span = slice(part * columns, (part + 1) * columns)
        enc_ref[:, span] = lax.dot_general(
            in_ref[...], grad, (((0,), (0,)), ((), ())), preferred_element_type=F32
        ).astype(BF16)
        bias_ref[:, span] = jnp.sum(grad.astype(F32), axis=0, keepdims=True)


def encoder_grads(local_in, pre_grad):
    tokens, rows = local_in.shape
    parts, _, columns = pre_grad.shape
    step = 8
    return pl.pallas_call(
        encoder_grad_kernel,
        grid=(parts // step,),
        in_specs=[
            pl.BlockSpec((tokens, rows), lambda c: (0, 0)),
            pl.BlockSpec((step, tokens, columns), lambda c: (c, 0, 0)),
        ],
        out_specs=[
            pl.BlockSpec((rows, step * columns), lambda c: (0, c)),
            pl.BlockSpec((1, step * columns), lambda c: (0, c)),
        ],
        out_shape=(
            jax.ShapeDtypeStruct((rows, parts * columns), BF16),
            jax.ShapeDtypeStruct((1, parts * columns), F32),
        ),
        name="encoder_grads",
    )(local_in, pre_grad)


TARGET = 0
LANES = ((4, 2), (3, 6), (5, 1), (7, 8, 0))


def on_device(inputs, encoder, enc_bias, active_blocks, near_decoders, far_decoders, targets):
    parts = lax.axis_size("width") // HALVES
    slots = near_decoders.shape[1]
    place = lax.axis_index("blk")[None].astype(jnp.int32)
    column = lax.axis_index("width") % parts
    local_in = inputs[0]
    near, far = near_decoders[0], far_decoders[0]
    columns = encoder.shape[2] // parts
    per_part = columns // FBLK
    blocks = lax.dynamic_slice_in_dim(active_blocks[0], column * per_part, per_part, 1)
    bias = lax.dynamic_slice_in_dim(enc_bias, column * columns, columns, 1)

    first = [near[lane[0]] for lane in LANES]
    first, rest = lax.optimization_barrier((first, near))
    moved = {}
    away_target = targets[0]
    for lane, slot in zip(LANES, first):
        before = None
        for o in lane:
            if before is None:
                moved[o] = shifted_down(slot, o)
            elif o == TARGET:
                away_target, moved[before] = lax.optimization_barrier((away_target, moved[before]))
                away_target = other_half(away_target)
            else:
                slot, moved[before] = lax.optimization_barrier(
                    (far if o == slots else rest[o], moved[before])
                )
                moved[o] = shifted_down(slot, o)
            before = o
    parted = pre_parts(local_in, encoder[0], parts)

    acts = summed_over_width(parted, bias, blocks)
    moved = [moved[o] for o in OPERANDS]
    shares = forward_shares(place, acts, near, far, moved)
    shares, away_target = lax.optimization_barrier((shares, away_target))
    own, other, sent = share_sums(place, exchange(shares, "blk"))
    reconstruction, own_grads = residual(
        place, own, other, other_half(sent), targets[0], away_target
    )
    all_grads = exchange(own_grads, "blk")
    all_parts = lax.axis_size("width")
    grad_parts = backward_parts(place, all_grads, near, far, moved, all_parts)
    few = active_blocks.shape[2] // all_parts
    own_blocks = lax.dynamic_slice_in_dim(
        active_blocks[0], lax.axis_index("width") * few, few, 1
    )
    pre_part = masked_total(exchange(grad_parts, "width"), own_blocks)
    pre_grad = exchange(pre_part, "width")
    enc_grad, bias_grad = encoder_grads(local_in, pre_grad)
    return reconstruction[None], enc_grad[None], bias_grad


def solution(mesh):
    return jax.shard_map(
        on_device,
        mesh=mesh,
        in_specs=(
            P("blk", None, "width"),
            P("blk", "width", None),
            P("blk", None),
            P("blk", None, None),
            P("blk", None, None, "width"),
            P("blk", None, "width"),
            P("blk", None, "width"),
        ),
        out_specs=(P("blk", None, "width"), P("blk", "width", None), P("blk", None)),
        check_vma=False,
    )
```
